256 devices in a mesh: space: 16 (over x, y), chan: 4 (over z_lo, core), filt: 4 (over z_hi).
Axes of the slice: x: 4, y: 4, z: 8 (z_hi: 4, z_lo: 2; z = z_hi * 2 + z_lo), core: 2. Of those that a mesh axis runs over, the one named last changes fastest.
Arguments:
- field: float32 [256, 4, 128, 256], P('chan', 'filt', 'space'), may hold values from -6 to 6
- weight: float32 [3, 3, 3, 256, 256], P(None, None, None, 'chan'), may hold values from -0.078125 to 0.078125
- bias: float32 [256], P('filt'), may hold values from -0.5 to 0.5
Outputs:
- output: float32 [256, 4, 128, 256], P('filt', 'chan', 'space')
The draws below stay inside these ranges and needn't reach their ends.
All inputs are finite; a program needn't handle non-finite values.
Results may differ from the reference program's by a relative error of at most 0.000073.
Values sent between devices are 32-bit elements; how exact they have to be, the bound alone decides.
A program may use at most 64 MiB of HBM per device.

```python
import jax
import jax.numpy as jnp
from jax import lax

CIN = 256
COUT = 256
NY = 256
NZ = 4
NX = 128


def block_scale(key, dims, pieces, low, top_value):
    loudness, own = 1.0, jax.random.fold_in(key, 6)
    for position, parts in pieces:
        steps = jnp.exp(jax.random.uniform(jax.random.fold_in(own, position), (parts,), jnp.float32, low / len(pieces), top_value / len(pieces)))
        loudness = loudness * jnp.repeat(steps, dims[position] // parts).reshape([-1 if axis == position else 1 for axis in range(len(dims))])
    return loudness


def normal_values(own_key, shape, width, reach, pieces=(), dtype=jnp.bfloat16):
    loudness = block_scale(own_key, shape, pieces, -0.22, 0.18) if pieces else 1.0
    result = jax.random.normal(own_key, shape, jnp.float32) * width * loudness
    return jnp.minimum(jnp.maximum(result, -reach), reach).astype(dtype)


def setup_inputs(seed: int = 0) -> dict:
    seeds = jax.random.split(jax.random.key(seed), 4)
    field = normal_values(seeds[0], (CIN, NZ, NX, NY), 1.0, 6.0, ((0, 4), (1, 4), (2, 16)), jnp.float32)
    weight = normal_values(seeds[1], (3, 3, 3, CIN, COUT), (27 * CIN) ** -0.5, 0.078125, ((3, 4),), jnp.float32)
    bias = jnp.clip(jax.random.uniform(seeds[2], (COUT,), jnp.float32, -0.5, 0.5) * block_scale(seeds[2], (COUT,), ((0, 4),), -0.4, 0.0), -0.5, 0.5)
    return dict(field=field, weight=weight, bias=bias)


def reference(field, weight, bias):
    kernel = jnp.transpose(weight, (4, 3, 0, 1, 2))
    pre = lax.conv_general_dilated(field[None], kernel, (1, 1, 1), ((1, 1), (1, 1), (1, 1)), dimension_numbers=("NCDHW", "OIDHW", "NCDHW"), precision=lax.Precision.HIGHEST, preferred_element_type=jnp.float32)[0]
    return jax.nn.silu(pre + bias[:, None, None, None])
```

```python
import jax
import jax.numpy as jnp
from jax import lax
from jax.experimental import pallas as pl
from jax.experimental.pallas import tpu as pltpu
from jax.sharding import PartitionSpec as P

MESH = pl.DeviceIdType.MESH
CHUNKS = ((0, 7, 0), (7, 7, 1), (14, 7, 0), (21, 6, 1))
F32, BF16 = jnp.float32, jnp.bfloat16


def split(value):
    high = value.astype(BF16)
    return high, (value - high.astype(F32)).astype(BF16)


def kernel(
    f_ref, w_ref, b_ref, o_ref,
    turned, out_in, got_in, cells, taps, weight_own, weight_other, wcat, total, sibling, out_back, got_back,
    own_sem, swap_ss, swap_rs, a_ss, a_rs, b_ss, b_rs, in_ss, in_rs, halo_ss, halo_rs, sib_ss, sib_rs, back_ss, back_rs,
):
    s, c, h = lax.axis_index("space"), lax.axis_index("chan"), lax.axis_index("filt")
    xx, yy = s // 4, s % 4
    lo, core = c // 2, c % 2
    z = 2 * h + lo

    def column(other_z, other_core):
        return (s, (other_z % 2) * 2 + other_core, other_z // 2)

    def plane(other_x, other_y):
        return (other_x * 4 + other_y, c, h)

    own = pltpu.make_async_copy(w_ref, weight_own, own_sem)
    own.start()

    barrier = pltpu.get_barrier_semaphore()
    greet = []
    for dz in range(8):
        for dk in range(2):
            if dz or dk:
                greet.append(column((z + dz) % 8, (core + dk) % 2))
    for d in range(1, 4):
        greet.append(plane((xx + d) % 4, yy))
        greet.append(plane(xx, (yy + d) % 4))
    greet.append(((s + 1) % 16, c, h))
    greet.append(((s + 15) % 16, c, h))
    for device in greet:
        pl.semaphore_signal(barrier, 1, device_id=device, device_id_type=MESH)
    pl.semaphore_wait(barrier, len(greet))

    def piece(ref, first, count, turn):
        u, v = (yy, xx) if turn else (xx, yy)
        rows = pl.multiple_of(16 * u + 8 * (v // 2), 8)
        lanes = pl.multiple_of(128 * (v % 2), 128)
        return ref.at[pl.ds(first, count), pl.ds(rows, 8), pl.ds(lanes, 128)]

    def band(ref, first, count, turn):
        u = yy if turn else xx
        return ref.at[pl.ds(first, count), pl.ds(pl.multiple_of(16 * u, 16), 16), :]

    swaps = []
    for q, (first, count, turn) in enumerate(CHUNKS):
        target = column((z + (7 if turn else 1)) % 8, core)
        swaps.append(
            pltpu.make_async_remote_copy(
                piece(w_ref, first, count, turn), piece(weight_other, first, count, turn),
                swap_ss.at[q], swap_rs.at[q], device_id=target, device_id_type=MESH,
            )
        )
        swaps[-1].start()

    lane = lax.broadcasted_iota(jnp.int32, (1, 128), 1)
    left = lane < 64
    for x in range(8):
        rows = f_ref[:, x, :]
        turned[x, 8:264, :] = jnp.concatenate([rows, rows], axis=0).T
        turned[x, 0:8, :] = jnp.zeros((8, 128), F32)
        turned[x, 264:272, :] = jnp.zeros((8, 128), F32)
    for t in range(8):
        base = 8 + 32 * t
        for x in range(8):
            out_in[t, 16 * x : 16 * x + 16, :] = jnp.where(
                left, turned[x, base : base + 16, :], turned[x, base + 16 : base + 32, :]
            )
        low_side = turned[:, base - 8 : base, :][:, 7, :]
        high_side = turned[:, base + 32 : base + 40, :][:, 0, :]
        out_in[t, 128:136, :] = jnp.where(left, low_side, high_side)
    ins = []
    for n, dz in enumerate((4, 3, 5, 2, 6, 1, 7)):
        target = (z + dz) % 8
        ins.append(
            pltpu.make_async_remote_copy(
                out_in.at[target], got_in.at[z], in_ss.at[n], in_rs.at[z],
                device_id=column(target, core), device_id_type=MESH,
            )
        )
        ins[-1].start()
    got_in[z] = out_in[z]

    @pl.when(s == 0)
    def _():
        cells[:, 0, :, :] = jnp.zeros((4, 48, 128), F32)

    @pl.when(s == 15)
    def _():
        cells[:, 9, :, :] = jnp.zeros((4, 48, 128), F32)

    spread_a, spread_b = [], []
    for q, (first, count, turn) in enumerate(CHUNKS):
        swaps[q].wait_recv()
        for d in range(1, 4):
            target = plane((xx + d) % 4, yy) if turn else plane(xx, (yy + d) % 4)
            block = piece(weight_other, first, count, turn)
            copy = pltpu.make_async_remote_copy(
                block, block, a_ss.at[q, d - 1], a_rs.at[q, d - 1], device_id=target, device_id_type=MESH
            )
            copy.start()
            spread_a.append(copy)
    for q, (first, count, turn) in enumerate(CHUNKS):
        for d in range(3):
            spread_a[3 * q + d].wait_recv()
        for d in range(1, 4):
            target = plane(xx, (yy + d) % 4) if turn else plane((xx + d) % 4, yy)
            block = band(weight_other, first, count, turn)
            copy = pltpu.make_async_remote_copy(
                block, block, b_ss.at[q, d - 1], b_rs.at[q, d - 1], device_id=target, device_id_type=MESH
            )
            copy.start()
            spread_b.append(copy)

    def convert(source, half, first, count):
        @pl.loop(first, first + count)
        def _(tap):
            ab, y = tap // 3, tap % 3
            high, low = split(source[tap])
            for place, value in ((256 * y, high), (256 * y + 128, high), (768 + 128 * y, low)):
                wcat[ab, pl.ds(pl.multiple_of(place + 64 * half, 64), 64), :] = value

    own.wait()
    convert(weight_own, lo, 0, 27)

    for n, dz in enumerate((7, 1, 6, 2, 5, 3, 4)):
        source = (z + dz) % 8
        pltpu.make_async_remote_copy(
            out_in.at[z], got_in.at[source], in_ss.at[n], in_rs.at[source],
            device_id=column(source, core), device_id_type=MESH,
        ).wait_recv()

    @pl.loop(0, 4)
    def _(p):
        for x in range(8):
            first = got_in[2 * p, 16 * x : 16 * x + 16, :]
            second = got_in[2 * p + 1, 16 * x : 16 * x + 16, :]
            cells[p, 1 + x, 8:24, :] = jnp.where(left, first, pltpu.roll(second, 64, 1))
            cells[p, 1 + x, 24:40, :] = jnp.where(left, pltpu.roll(first, 64, 1), second)
        first = got_in[2 * p, 128:136, :]
        second = got_in[2 * p + 1, 128:136, :]
        low_side = jnp.where(left, first, pltpu.roll(second, 64, 1))
        high_side = jnp.where(left, pltpu.roll(first, 64, 1), second)
        for x in range(8):
            cells[p, 1 + x, 7:8, :] = low_side[x : x + 1]
            cells[p, 1 + x, 40:41, :] = high_side[x : x + 1]

    up = pltpu.make_async_remote_copy(
        cells.at[:, 8], cells.at[:, 0], halo_ss.at[0], halo_rs.at[0],
        device_id=((s + 1) % 16, c, h), device_id_type=MESH,
    )
    down = pltpu.make_async_remote_copy(
        cells.at[:, 1], cells.at[:, 9], halo_ss.at[1], halo_rs.at[1],
        device_id=((s + 15) % 16, c, h), device_id_type=MESH,
    )

    @pl.when(s < 15)
    def _():
        up.start()

    @pl.when(s > 0)
    def _():
        down.start()

    def spread(x):
        @pl.loop(0, 4)
        def _(p):
            for y in range(3):
                high, low = split(cells[p, x, 7 + y : 39 + y, :])
                taps[p, x, :, 256 * y : 256 * y + 128] = high
                taps[p, x, :, 256 * y + 128 : 256 * y + 256] = low
                taps[p, x, :, 768 + 128 * y : 896 + 128 * y] = high

    @pl.loop(1, 9)
    def _(x):
        spread(x)

    @pl.when(s > 0)
    def _():
        up.wait_recv()

    @pl.when(s < 15)
    def _():
        down.wait_recv()

    spread(0)
    spread(9)

    for copy in spread_b:
        copy.wait_recv()
    convert(weight_other, 1 - lo, 0, 27)

    def group(g, slot):
        edge, inner, far = 3 * g, 1 + g, 2 - g
        onward = 2 - 2 * g

        def left_side(p, b):
            return taps[p, pl.ds(b, 8)].reshape(256, 1152)

        for b in range(3):
            first, second, third = left_side(edge, b), left_side(inner, b), left_side(far, b)
            same = jnp.dot(
                jnp.concatenate([first, second], axis=0), wcat[3 + b], preferred_element_type=F32
            )
            if b == 0:
                total[slot] = same
            else:
                total[slot] += same
            total[slot] += jnp.dot(
                jnp.concatenate([second, third], axis=0), wcat[3 * onward + b], preferred_element_type=F32
            )
            total[slot, 256:512, :] += jnp.dot(first, wcat[3 * (2 - onward) + b], preferred_element_type=F32)

    group(1 - core, 0)
    exchange = pltpu.make_async_remote_copy(
        total.at[0], sibling, sib_ss, sib_rs, device_id=column(z, 1 - core), device_id_type=MESH
    )
    exchange.start()
    group(core, 1)
    exchange.wait_recv()

    for n in range(2):
        p = (3 * core, 1 + core)[n]
        for pair in range(2):
            rows, lanes = slice(256 * n, 256 * n + 256), slice(128 * pair, 128 * pair + 128)
            value = (total[1, rows, lanes] + sibling[rows, lanes]).reshape(8, 32, 128)
            low_part = value[:, :16, :].reshape(128, 128)
            high_part = value[:, 16:, :].reshape(128, 128)
            out_back[4 * n + 2 * pair] = jnp.where(left, low_part, pltpu.roll(high_part, 64, 1))
            out_back[4 * n + 2 * pair + 1] = jnp.where(left, pltpu.roll(low_part, 64, 1), high_part)
            for f in (2 * pair, 2 * pair + 1):
                here = jnp.logical_and(p == c, f == h)
                block = 4 * n + f

                @pl.when(here)
                def _():
                    pltpu.make_async_copy(out_back.at[block], got_back.at[z], back_rs.at[z]).start()

                @pl.when(jnp.logical_not(here))
                def _():
                    pltpu.make_async_remote_copy(
                        out_back.at[block], got_back.at[z], back_ss.at[block], back_rs.at[z],
                        device_id=(s, p, f), device_id_type=MESH,
                    ).start()

    for source in range(8):
        pltpu.make_async_copy(got_back.at[source], got_back.at[source], back_rs.at[source]).wait()

    bias = b_ref[...].reshape(1, 64)
    bias = jnp.concatenate([bias, bias], axis=1)
    for x in range(8):
        value = got_back[:, 16 * x : 16 * x + 16, :] + bias.reshape(1, 1, 128)
        value = value / (1.0 + jnp.exp(-value))
        value = value.reshape(128, 128)
        other = pltpu.roll(value, 64, 1)
        rows = jnp.stack([value.reshape(8, 16, 128), other.reshape(8, 16, 128)], axis=1).reshape(256, 128)
        o_ref[:, x, :] = rows.T[:64, :]

    for copy in swaps + spread_a + spread_b + ins + [exchange]:
        copy.wait_send()

    @pl.when(s < 15)
    def _():
        up.wait_send()

    @pl.when(s > 0)
    def _():
        down.wait_send()

    for n in range(2):
        p = (3 * core, 1 + core)[n]
        for f in range(4):
            block = 4 * n + f

            @pl.when(jnp.logical_not(jnp.logical_and(p == c, f == h)))
            def _():
                pltpu.make_async_remote_copy(
                    out_back.at[block], got_back.at[z], back_ss.at[block], back_rs.at[z],
                    device_id=(s, p, f), device_id_type=MESH,
                ).wait_send()


def per_device(field, weight, bias):
    dma, chunks = pltpu.SemaphoreType.DMA, len(CHUNKS)
    result = pl.pallas_call(
        kernel,
        out_shape=jax.ShapeDtypeStruct((64, 8, 256), F32),
        in_specs=[
            pl.BlockSpec(memory_space=pltpu.VMEM),
            pl.BlockSpec(memory_space=pl.ANY),
            pl.BlockSpec(memory_space=pltpu.VMEM),
        ],
        out_specs=pl.BlockSpec(memory_space=pltpu.VMEM),
        scratch_shapes=[
            pltpu.VMEM((8, 272, 128), F32),
            pltpu.VMEM((8, 136, 128), F32),
            pltpu.VMEM((8, 136, 128), F32),
            pltpu.VMEM((4, 10, 48, 128), F32),
            pltpu.VMEM((4, 10, 32, 1152), BF16),
            pltpu.VMEM((27, 64, 256), F32),
            pltpu.VMEM((27, 64, 256), F32),
            pltpu.VMEM((9, 1152, 256), BF16),
            pltpu.VMEM((2, 512, 256), F32),
            pltpu.VMEM((512, 256), F32),
            pltpu.VMEM((8, 128, 128), F32),
            pltpu.VMEM((8, 128, 128), F32),
            dma,
            dma((chunks,)),
            dma((chunks,)),
            dma((chunks, 3)),
            dma((chunks, 3)),
            dma((chunks, 3)),
            dma((chunks, 3)),
            dma((7,)),
            dma((8,)),
            dma((2,)),
            dma((2,)),
            dma,
            dma,
            dma((8,)),
            dma((8,)),
        ],
        compiler_params=pltpu.CompilerParams(
            collective_id=0, has_side_effects=True, vmem_limit_bytes=48 * 2**20
        ),
        cost_estimate=pl.CostEstimate(flops=4 * 10**9, bytes_accessed=4 * 10**6, transcendentals=131072),
        name="convolution",
    )(field.reshape(64, 8, 256), weight.reshape(27, 64, 256), bias)
    return result.reshape(64, 1, 8, 256)


def solution(mesh):
    placed = (P("chan", "filt", "space", None), P(None, None, None, "chan", None), P("filt"))
    return jax.shard_map(
        per_device,
        mesh=mesh,
        in_specs=placed,
        out_specs=P("filt", "chan", "space", None),
        check_vma=False,
    )
```

```python
import jax
import jax.numpy as jnp
from jax import lax
from jax.experimental import pallas as pl
from jax.experimental.pallas import tpu as pltpu
from jax.sharding import PartitionSpec as P

MESH = pl.DeviceIdType.MESH
CHUNKS = ((9, 5, 0), (14, 4, 1), (0, 4, 0), (4, 5, 1), (18, 5, 0), (23, 4, 1))
NEAR = (1, 7, 2, 6, 3, 5, 4)
ORDER = (0, 7, 1, 2, 3, 4, 5, 6)
F32, BF16 = jnp.float32, jnp.bfloat16


def split(value):
    high = value.astype(BF16)
    return high, (value - high.astype(F32)).astype(BF16)


def kernel(
    f_ref, w_ref, b_ref, o_ref,
    field, bias, turned, out_in, got_in, cells, taps, weight_own, weight_other, wcat, total, sibling, out_back, got_back, ready,
    own_sem, swap_ss, swap_rs, a_ss, a_rs, b_ss, b_rs, in_ss, in_rs, halo_ss, halo_rs, sib_ss, sib_rs, back_ss, back_rs,
):
    s, c, h = lax.axis_index("space"), lax.axis_index("chan"), lax.axis_index("filt")
    xx, yy = s // 4, s % 4
    lo, core = c // 2, c % 2
    z = 2 * h + lo

    def column(other_z, other_core):
        return (s, (other_z % 2) * 2 + other_core, other_z // 2)

    def plane(other_x, other_y):
        return (other_x * 4 + other_y, c, h)

    def remote(source, target, send, receive, device):
        return pltpu.make_async_remote_copy(
            source, target, send, receive, device_id=device, device_id_type=MESH
        )

    fetch_field = pltpu.make_async_copy(f_ref, field, own_sem.at[0])
    fetch_field.start()

    barrier = pltpu.get_barrier_semaphore()
    greet = []
    for dz in range(8):
        for dk in range(2):
            if dz or dk:
                greet.append(column((z + dz) % 8, (core + dk) % 2))
    for d in range(1, 4):
        greet.append(plane((xx + d) % 4, yy))
        greet.append(plane(xx, (yy + d) % 4))
    greet.append(((s + 1) % 16, c, h))
    greet.append(((s + 15) % 16, c, h))
    for device in greet:
        pl.semaphore_signal(barrier, 1, device_id=device, device_id_type=MESH)
    fetch_weight = pltpu.make_async_copy(w_ref, weight_own, own_sem.at[1])
    fetch_weight.start()
    fetch_bias = pltpu.make_async_copy(b_ref, bias, own_sem.at[2])
    fetch_bias.start()

    lane = lax.broadcasted_iota(jnp.int32, (1, 128), 1)
    left = lane < 64
    fetch_field.wait()
    for x in range(8):
        rows = field[:, x, :]
        turned[x, 8:264, :] = jnp.concatenate([rows, rows], axis=0).T
        turned[x, 0:8, :] = jnp.zeros((8, 128), F32)
        turned[x, 264:272, :] = jnp.zeros((8, 128), F32)
    for t in range(8):
        base = 8 + 32 * t
        low_side = turned[:, base - 8 : base, :][:, 7, :]
        high_side = turned[:, base + 32 : base + 40, :][:, 0, :]
        out_in[t, 0:8, :] = jnp.where(left, low_side, high_side)
        for n, x in enumerate(ORDER):
            out_in[t, 8 + 16 * n : 24 + 16 * n, :] = jnp.where(
                left, turned[x, base : base + 16, :], turned[x, base + 16 : base + 32, :]
            )
    got_in[z] = out_in[z]

    @pl.when(s == 0)
    def _():
        cells[:, 0, :, :] = jnp.zeros((4, 48, 128), F32)

    @pl.when(s == 15)
    def _():
        cells[:, 9, :, :] = jnp.zeros((4, 48, 128), F32)

    pl.semaphore_wait(barrier, len(greet))

    def piece(ref, first, count, turn):
        u, v = (yy, xx) if turn else (xx, yy)
        rows = pl.multiple_of(16 * u + 8 * (v // 2), 8)
        lanes = pl.multiple_of(128 * (v % 2), 128)
        return ref.at[pl.ds(first, count), pl.ds(rows, 8), pl.ds(lanes, 128)]

    def band(ref, first, count, turn):
        u = yy if turn else xx
        return ref.at[pl.ds(first, count), pl.ds(pl.multiple_of(16 * u, 16), 16), :]

    swaps = []
    for q, (first, count, turn) in enumerate(CHUNKS):
        target = column((z + (7 if turn else 1)) % 8, core)
        swaps.append(
            remote(
                piece(w_ref, first, count, turn), piece(weight_other, first, count, turn),
                swap_ss.at[q], swap_rs.at[q], target,
            )
        )
        swaps[-1].start()

    PARTS = (pl.ds(0, 40), pl.ds(40, 96))
    ins = []
    for part in range(2):
        for n, dz in enumerate(NEAR):
            target = (z + dz) % 8
            ins.append(
                remote(
                    out_in.at[target, PARTS[part]], got_in.at[z, PARTS[part]],
                    in_ss.at[part, n], in_rs.at[part, z], column(target, core),
                )
            )
            ins[-1].start()

    def convert(source, half, first, count):
        @pl.loop(first, first + count)
        def _(tap):
            ab, y = tap // 3, tap % 3
            high, low = split(source[tap])
            for place, value in ((256 * y, high), (256 * y + 128, high), (768 + 128 * y, low)):
                wcat[ab, pl.ds(pl.multiple_of(place + 64 * half, 64), 64), :] = value

    fetch_weight.wait()
    convert(weight_own, lo, 0, 13)

    spread_a, spread_b = [], []
    for q, (first, count, turn) in enumerate(CHUNKS):
        swaps[q].wait_recv()
        for d in range(1, 4):
            target = plane((xx + d) % 4, yy) if turn else plane(xx, (yy + d) % 4)
            block = piece(weight_other, first, count, turn)
            copy = remote(block, block, a_ss.at[q, d - 1], a_rs.at[q, d - 1], target)
            copy.start()
            spread_a.append(copy)
    convert(weight_own, lo, 13, 14)
    for q, (first, count, turn) in enumerate(CHUNKS):
        for d in range(3):
            spread_a[3 * q + d].wait_recv()
        for d in range(1, 4):
            target = plane(xx, (yy + d) % 4) if turn else plane((xx + d) % 4, yy)
            block = band(weight_other, first, count, turn)
            copy = remote(block, block, b_ss.at[q, d - 1], b_rs.at[q, d - 1], target)
            copy.start()
            spread_b.append(copy)

    def arrived(part, p):
        for l in range(2):
            source = 2 * p + l

            @pl.when(source != z)
            def _():
                remote(
                    out_in.at[z, PARTS[part]], got_in.at[source, PARTS[part]],
                    in_ss.at[part, 0], in_rs.at[part, source], column(source, core),
                ).wait_recv()

    def unpack(p, n):
        x = ORDER[n]
        first = got_in[2 * p, 8 + 16 * n : 24 + 16 * n, :]
        second = got_in[2 * p + 1, 8 + 16 * n : 24 + 16 * n, :]
        cells[p, 1 + x, 8:24, :] = jnp.where(left, first, pltpu.roll(second, 64, 1))
        cells[p, 1 + x, 24:40, :] = jnp.where(left, pltpu.roll(first, 64, 1), second)

    def spread(p, x):
        for y in range(3):
            high, low = split(cells[p, x, 7 + y : 39 + y, :])
            taps[p, x, :, 256 * y : 256 * y + 128] = high
            taps[p, x, :, 256 * y + 128 : 256 * y + 256] = low
            taps[p, x, :, 768 + 128 * y : 896 + 128 * y] = high

    def boundary(p):
        arrived(0, p)
        first = got_in[2 * p, 0:8, :]
        second = got_in[2 * p + 1, 0:8, :]
        low_side = jnp.where(left, first, pltpu.roll(second, 64, 1))
        high_side = jnp.where(left, pltpu.roll(first, 64, 1), second)
        for x in range(8):
            cells[p, 1 + x, 7:8, :] = low_side[x : x + 1]
            cells[p, 1 + x, 40:41, :] = high_side[x : x + 1]
        unpack(p, 0)
        unpack(p, 1)

    def inside(p):
        arrived(1, p)
        for n in range(2, 8):
            unpack(p, n)

        @pl.loop(1, 9)
        def _(x):
            spread(p, x)

    planes = [(h + d) % 4 for d in (0, 1, 3, 2)]

    @pl.loop(0, 4)
    def _(n):
        boundary((h + n) % 4)

    up = remote(cells.at[:, 8], cells.at[:, 0], halo_ss.at[0], halo_rs.at[0], ((s + 1) % 16, c, h))
    down = remote(cells.at[:, 1], cells.at[:, 9], halo_ss.at[1], halo_rs.at[1], ((s + 15) % 16, c, h))

    @pl.when(s < 15)
    def _():
        up.start()

    @pl.when(s > 0)
    def _():
        down.start()

    for p in planes:
        inside(p)

    @pl.when(s > 0)
    def _():
        up.wait_recv()

    @pl.when(s < 15)
    def _():
        down.wait_recv()

    @pl.loop(0, 4)
    def _(p):
        spread(p, 0)
        spread(p, 9)

    for q, (first, count, turn) in enumerate(CHUNKS):
        for d in range(3):
            spread_b[3 * q + d].wait_recv()
        convert(weight_other, 1 - lo, first, count)

    def left_side(p):
        return jnp.concatenate([taps[p, pl.ds(b, 8)].reshape(256, 1152) for b in range(3)], axis=1)

    def right_side(a):
        return wcat[pl.ds(3 * a, 3)].reshape(3456, 256)

    def convolve(g, inner):
        near, far, onward = 3 * g, 2 - g, 2 - 2 * g
        if inner:
            terms = ((near, 2 - onward), (1 + g, 1), (far, onward))
        else:
            terms = ((near, 1), (1 + g, onward))
        return jnp.dot(
            jnp.concatenate([left_side(p) for p, _ in terms], axis=1),
            jnp.concatenate([right_side(a) for _, a in terms], axis=0),
            preferred_element_type=F32,
        )

    exchanges, backs = [], []
    for inner in range(2):
        total[inner] = convolve(1 - core, inner)
        exchange = remote(
            total.at[inner], sibling.at[inner], sib_ss.at[inner], sib_rs.at[inner], column(z, 1 - core)
        )
        exchange.start()
        exchanges.append(exchange)
        total[2 + inner] = convolve(core, inner)
        exchange.wait_recv()

        p = 1 + core if inner else 3 * core
        for pair in range(2):
            lanes = slice(128 * pair, 128 * pair + 128)
            value = (total[2 + inner, :, lanes] + sibling[inner, :, lanes]).reshape(8, 32, 128)
            low_part = value[:, :16, :].reshape(128, 128)
            high_part = value[:, 16:, :].reshape(128, 128)
            out_back[inner, 2 * pair] = jnp.where(left, low_part, pltpu.roll(high_part, 64, 1))
            out_back[inner, 2 * pair + 1] = jnp.where(left, pltpu.roll(low_part, 64, 1), high_part)
        for d in (2, 1, 3, 0):
            f = (h + d) % 4
            copy = remote(
                out_back.at[inner, f], got_back.at[z], back_ss.at[inner, d], back_rs.at[z], (s, p, f)
            )
            if d == 0:
                here = pltpu.make_async_copy(out_back.at[inner, f], got_back.at[z], back_rs.at[z])

                @pl.when(p == c)
                def _():
                    here.start()

                @pl.when(p != c)
                def _():
                    copy.start()
            else:
                copy.start()
            backs.append((copy, p, d))

    fetch_bias.wait()
    offset = bias[...].reshape(1, 64)
    offset = jnp.concatenate([offset, offset], axis=1)
    for n in range(8):
        source = (z + (0, 1, 7, 2, 6, 3, 5, 4)[n]) % 8
        pltpu.make_async_copy(got_back.at[source], got_back.at[source], back_rs.at[source]).wait()
        value = got_back[source] + offset
        value = value / (1.0 + jnp.exp(-value))
        rows = pl.multiple_of(32 * source, 32)
        ready[:, pl.ds(rows, 16), :] = value.reshape(8, 16, 128)
        ready[:, pl.ds(rows + 16, 16), :] = pltpu.roll(value, 64, 1).reshape(8, 16, 128)
    for x in range(8):
        o_ref[:, x, :] = ready[x].T[:64, :]

    for copy in swaps + spread_a + spread_b + ins + exchanges:
        copy.wait_send()

    @pl.when(s < 15)
    def _():
        up.wait_send()

    @pl.when(s > 0)
    def _():
        down.wait_send()

    for copy, p, d in backs:
        if d == 0:
            @pl.when(p != c)
            def _():
                copy.wait_send()
        else:
            copy.wait_send()


def per_device(field, weight, bias):
    dma, chunks = pltpu.SemaphoreType.DMA, len(CHUNKS)
    result = pl.pallas_call(
        kernel,
        out_shape=jax.ShapeDtypeStruct((64, 8, 256), F32),
        in_specs=[pl.BlockSpec(memory_space=pltpu.HBM)] * 3,
        out_specs=pl.BlockSpec(memory_space=pltpu.VMEM),
        scratch_shapes=[
            pltpu.VMEM((64, 8, 256), F32),
            pltpu.VMEM((64,), F32),
            pltpu.VMEM((8, 272, 128), F32),
            pltpu.VMEM((8, 136, 128), F32),
            pltpu.VMEM((8, 136, 128), F32),
            pltpu.VMEM((4, 10, 48, 128), F32),
            pltpu.VMEM((4, 10, 32, 1152), BF16),
            pltpu.VMEM((27, 64, 256), F32),
            pltpu.VMEM((27, 64, 256), F32),
            pltpu.VMEM((9, 1152, 256), BF16),
            pltpu.VMEM((4, 256, 256), F32),
            pltpu.VMEM((2, 256, 256), F32),
            pltpu.VMEM((2, 4, 128, 128), F32),
            pltpu.VMEM((8, 128, 128), F32),
            pltpu.VMEM((8, 256, 128), F32),
            dma((3,)),
            dma((chunks,)),
            dma((chunks,)),
            dma((chunks, 3)),
            dma((chunks, 3)),
            dma((chunks, 3)),
            dma((chunks, 3)),
            dma((2, 7)),
            dma((2, 8)),
            dma((2,)),
            dma((2,)),
            dma((2,)),
            dma((2,)),
            dma((2, 4)),
            dma((8,)),
        ],
        compiler_params=pltpu.CompilerParams(
            collective_id=0, has_side_effects=True, vmem_limit_bytes=63 * 2**20
        ),
        cost_estimate=pl.CostEstimate(flops=4 * 10**9, bytes_accessed=4 * 10**6, transcendentals=131072),
        name="convolution",
    )(field.reshape(64, 8, 256), weight.reshape(27, 64, 256), bias)
    return result.reshape(64, 1, 8, 256)


def solution(mesh):
    placed = (P("chan", "filt", "space", None), P(None, None, None, "chan", None), P("filt"))
    return jax.shard_map(
        per_device,
        mesh=mesh,
        in_specs=placed,
        out_specs=P("filt", "chan", "space", None),
        check_vma=False,
    )
```

```python
import jax
import jax.numpy as jnp
from jax import lax
from jax.experimental import pallas as pl
from jax.experimental.pallas import tpu as pltpu
from jax.sharding import PartitionSpec as P

MESH = pl.DeviceIdType.MESH
CHUNKS = ((0, 8, 0), (14, 8, 1), (8, 6, 0), (22, 6, 1))
NEAR = (1, 7, 2, 6, 3, 5, 4)
ORDER = (0, 7, 1, 2, 3, 4, 5, 6)
F32, BF16 = jnp.float32, jnp.bfloat16


def split(value):
    high = value.astype(BF16)
    return high, (value - high.astype(F32)).astype(BF16)


def kernel(
    f_ref, w_ref, b_ref, o_ref,
    field, bias, turned, out_in, got_in, cells, taps, weight_own, weight_other, wcat, total, sibling, out_back, got_back, ready,
    own_sem, swap_ss, swap_rs, a_ss, a_rs, b_ss, b_rs, in_ss, in_rs, halo_ss, halo_rs, sib_ss, sib_rs, back_ss, back_rs,
):
    s, c, h = lax.axis_index("space"), lax.axis_index("chan"), lax.axis_index("filt")
    xx, yy = s // 4, s % 4
    lo, core = c // 2, c % 2
    z = 2 * h + lo

    def column(other_z, other_core):
        return (s, (other_z % 2) * 2 + other_core, other_z // 2)

    def plane(other_x, other_y):
        return (other_x * 4 + other_y, c, h)

    def remote(source, target, send, receive, device):
        return pltpu.make_async_remote_copy(
            source, target, send, receive, device_id=device, device_id_type=MESH
        )

    fetch_field = pltpu.make_async_copy(f_ref, field, own_sem.at[0])
    fetch_field.start()

    barrier = pltpu.get_barrier_semaphore()
    greet = []
    for dz in range(8):
        for dk in range(2):
            if dz or dk:
                greet.append(column((z + dz) % 8, (core + dk) % 2))
    for d in range(1, 4):
        greet.append(plane((xx + d) % 4, yy))
        greet.append(plane(xx, (yy + d) % 4))
    greet.append(((s + 1) % 16, c, h))
    greet.append(((s + 15) % 16, c, h))
    for device in greet:
        pl.semaphore_signal(barrier, 1, device_id=device, device_id_type=MESH)
    fetch_weight = pltpu.make_async_copy(w_ref, weight_own.at[pl.ds(0, 27)], own_sem.at[1])
    fetch_weight.start()
    fetch_bias = pltpu.make_async_copy(b_ref, bias, own_sem.at[2])
    fetch_bias.start()

    lane = lax.broadcasted_iota(jnp.int32, (1, 128), 1)
    left = lane < 64
    fetch_field.wait()
    for x in range(8):
        rows = field[:, x, :]
        turned[x, 8:264, :] = jnp.concatenate([rows, rows], axis=0).T
        turned[x, 0:8, :] = jnp.zeros((8, 128), F32)
        turned[x, 264:272, :] = jnp.zeros((8, 128), F32)
    for t in range(8):
        base = 8 + 32 * t
        low_side = turned[:, base - 8 : base, :][:, 7, :]
        high_side = turned[:, base + 32 : base + 40, :][:, 0, :]
        out_in[t, 0:8, :] = jnp.where(left, low_side, high_side)
        for n, x in enumerate(ORDER):
            out_in[t, 8 + 16 * n : 24 + 16 * n, :] = jnp.where(
                left, turned[x, base : base + 16, :], turned[x, base + 16 : base + 32, :]
            )
    got_in[z] = out_in[z]

    @pl.when(s == 0)
    def _():
        cells[:, 0, :, :] = jnp.zeros((4, 48, 128), F32)

    @pl.when(s == 15)
    def _():
        cells[:, 9, :, :] = jnp.zeros((4, 48, 128), F32)

    pl.semaphore_wait(barrier, len(greet))

    def place(first, count, turn):
        u, v = (yy, xx) if turn else (xx, yy)
        rows = pl.multiple_of(16 * u + 8 * (v // 2), 8)
        return pl.ds(first + (count // 2) * (v % 2), count // 2), pl.ds(rows, 8)

    def piece(m, first, count, turn):
        own_taps, own_rows = place(first, count, turn)
        return weight_other.at[m, own_taps, own_rows, :]

    def band(m, first, count, turn):
        u = yy if turn else xx
        return weight_other.at[m, pl.ds(first, count), pl.ds(pl.multiple_of(16 * u, 16), 16), :]

    swaps = [[], []]

    def swap(m):
        for q, (first, count, turn) in enumerate(CHUNKS):
            target = (z + (7 if turn else 1)) % 8
            own_taps, own_rows = place(first, count, turn)
            lanes = pl.ds(pl.multiple_of(128 * ((target + m) % 2), 128), 128)
            copy = remote(
                weight_own.at[own_taps, own_rows, lanes], piece(m, first, count, turn),
                swap_ss.at[m, q], swap_rs.at[m, q], column(target, core),
            )
            copy.start()
            swaps[m].append(copy)

    weight_own[27] = jnp.zeros((64, 256), F32)
    fetch_weight.wait()
    swap(0)

    PARTS = (pl.ds(0, 40), pl.ds(40, 96))
    ins = []
    for part in range(2):
        for n, dz in enumerate(NEAR):
            target = (z + dz) % 8
            ins.append(
                remote(
                    out_in.at[target, PARTS[part]], got_in.at[z, PARTS[part]],
                    in_ss.at[part, n], in_rs.at[part, z], column(target, core),
                )
            )
            ins[-1].start()
        if part == 0:
            swap(1)

    def convert(m, half, first, count, read):
        @pl.loop(first, first + count)
        def _(tap):
            ab, y = tap // 3, tap % 3
            high, low = split(read(tap))
            for base, value in ((256 * y, high), (256 * y + 128, high), (768 + 128 * y, low)):
                wcat[m, ab, pl.ds(pl.multiple_of(base + 64 * half, 64), 64), :] = value

    for j in range(2):
        convert((j + lo) % 2, lo, 0, 27, lambda tap: weight_own[tap, :, 128 * j : 128 * j + 128])

    spread_a, spread_b = [[], []], [[], []]

    def gather_a(m):
        for q, (first, count, turn) in enumerate(CHUNKS):
            swaps[m][q].wait_recv()
            for d in range(1, 4):
                target = plane((xx + d) % 4, yy) if turn else plane(xx, (yy + d) % 4)
                block = piece(m, first, count, turn)
                copy = remote(block, block, a_ss.at[m, q, d - 1], a_rs.at[m, q, d - 1], target)
                copy.start()
                spread_a[m].append(copy)

    def gather_b(m):
        for q, (first, count, turn) in enumerate(CHUNKS):
            for d in range(3):
                spread_a[m][3 * q + d].wait_recv()
            for d in range(1, 4):
                target = plane(xx, (yy + d) % 4) if turn else plane((xx + d) % 4, yy)
                block = band(m, first, count, turn)
                copy = remote(block, block, b_ss.at[m, q, d - 1], b_rs.at[m, q, d - 1], target)
                copy.start()
                spread_b[m].append(copy)

    def gathered(m):
        for q, (first, count, turn) in enumerate(CHUNKS):
            for d in range(3):
                spread_b[m][3 * q + d].wait_recv()
            convert(m, 1 - lo, first, min(count, 27 - first), lambda tap: weight_other[m, tap])

    gather_a(0)
    gather_b(0)
    gather_a(1)

    def arrived(part, p):
        for l in range(2):
            source = 2 * p + l

            @pl.when(source != z)
            def _():
                remote(
                    out_in.at[z, PARTS[part]], got_in.at[source, PARTS[part]],
                    in_ss.at[part, 0], in_rs.at[part, source], column(source, core),
                ).wait_recv()

    def unpack(p, n):
        x = ORDER[n]
        first = got_in[2 * p, 8 + 16 * n : 24 + 16 * n, :]
        second = got_in[2 * p + 1, 8 + 16 * n : 24 + 16 * n, :]
        cells[p, 1 + x, 8:24, :] = jnp.where(left, first, pltpu.roll(second, 64, 1))
        cells[p, 1 + x, 24:40, :] = jnp.where(left, pltpu.roll(first, 64, 1), second)

    def spread(p, x):
        for y in range(3):
            high, low = split(cells[p, x, 7 + y : 39 + y, :])
            taps[p, x, :, 256 * y : 256 * y + 128] = high
            taps[p, x, :, 256 * y + 128 : 256 * y + 256] = low
            taps[p, x, :, 768 + 128 * y : 896 + 128 * y] = high

    def boundary(p):
        arrived(0, p)
        first = got_in[2 * p, 0:8, :]
        second = got_in[2 * p + 1, 0:8, :]
        low_side = jnp.where(left, first, pltpu.roll(second, 64, 1))
        high_side = jnp.where(left, pltpu.roll(first, 64, 1), second)
        for x in range(8):
            cells[p, 1 + x, 7:8, :] = low_side[x : x + 1]
            cells[p, 1 + x, 40:41, :] = high_side[x : x + 1]
        unpack(p, 0)
        unpack(p, 1)

    def inside(p):
        arrived(1, p)
        for n in range(2, 8):
            unpack(p, n)

        @pl.loop(1, 9)
        def _(x):
            spread(p, x)

    planes = [(h + d) % 4 for d in (0, 1, 3, 2)]

    @pl.loop(0, 4)
    def _(n):
        boundary((h + n) % 4)

    up = remote(cells.at[:, 8], cells.at[:, 0], halo_ss.at[0], halo_rs.at[0], ((s + 1) % 16, c, h))
    down = remote(cells.at[:, 1], cells.at[:, 9], halo_ss.at[1], halo_rs.at[1], ((s + 15) % 16, c, h))

    @pl.when(s < 15)
    def _():
        up.start()

    @pl.when(s > 0)
    def _():
        down.start()

    gather_b(1)
    gathered(0)
    for p in planes:
        inside(p)

    @pl.when(s > 0)
    def _():
        up.wait_recv()

    @pl.when(s < 15)
    def _():
        down.wait_recv()

    @pl.loop(0, 4)
    def _(p):
        spread(p, 0)
        spread(p, 9)

    def left_side(part, p):
        return jnp.concatenate([taps[p, pl.ds(4 * part + b, 4)].reshape(128, 1152) for b in range(3)], axis=1)

    def right_side(m, a):
        return wcat[m, pl.ds(3 * a, 3)].reshape(3456, 128)

    def convolve(target, part, m, g):
        onward = 2 - 2 * g
        middle, ahead = right_side(m, 1), right_side(m, onward)
        target[...] = jnp.dot(
            jnp.concatenate([left_side(part, 3 * g), left_side(part, 1 + g)], axis=1),
            jnp.concatenate(
                [
                    jnp.concatenate([middle, right_side(m, 2 - onward)], axis=1),
                    jnp.concatenate([ahead, middle], axis=1),
                ],
                axis=0,
            ),
            preferred_element_type=F32,
        )
        target[:, 128:] += jnp.dot(left_side(part, 2 - g), ahead, preferred_element_type=F32)

    exchanges, backs = [], []

    def begin(part, m):
        k = 2 * m + part
        convolve(total.at[k, 0], part, m, 1 - core)
        exchange = remote(total.at[k, 0], sibling.at[k], sib_ss.at[k], sib_rs.at[k], column(z, 1 - core))
        exchange.start()
        exchanges.append(exchange)

    def finish(part, m):
        k = 2 * m + part
        convolve(total.at[k, 1], part, m, core)
        exchanges[k].wait_recv()

        for n in range(2):
            p = 1 + core if n else 3 * core
            lanes = slice(128 * n, 128 * n + 128)
            value = (total[k, 1, :, lanes] + sibling[k, :, lanes]).reshape(4, 32, 128)
            low_part = value[:, :16, :].reshape(64, 128)
            high_part = value[:, 16:, :].reshape(64, 128)
            out_back[k, n, 0] = jnp.where(left, low_part, pltpu.roll(high_part, 64, 1))
            out_back[k, n, 1] = jnp.where(left, pltpu.roll(low_part, 64, 1), high_part)
            for j in range(2):
                f = 2 * ((lo + m) % 2) + j
                away = jnp.logical_or(p != c, f != h)
                block, place_back = out_back.at[k, n, j], got_back.at[z, part]
                copy = remote(block, place_back, back_ss.at[k, n, j], back_rs.at[z, part], (s, p, f))
                here = pltpu.make_async_copy(block, place_back, back_rs.at[z, part])
                pl.when(away)(copy.start)
                pl.when(jnp.logical_not(away))(here.start)
                backs.append((copy, away))

    for m in range(2):
        if m:
            gathered(m)
        begin(0, m)
        begin(1, m)
        finish(0, m)
        finish(1, m)

    fetch_bias.wait()
    offset = bias[...].reshape(1, 64)
    offset = jnp.concatenate([offset, offset], axis=1)
    for n in range(16):
        source, part = 2 * (n % 4) + (h // 2 + n // 8) % 2, n // 4 % 2
        arrival = got_back.at[source, part]
        pltpu.make_async_copy(arrival, arrival, back_rs.at[source, part]).wait()
        value = got_back[source, part] + offset
        value = value / (1.0 + jnp.exp(-value))
        rows, columns = pl.multiple_of(32 * source, 32), slice(4 * part, 4 * part + 4)
        ready[columns, pl.ds(rows, 16), :] = value.reshape(4, 16, 128)
        ready[columns, pl.ds(rows + 16, 16), :] = pltpu.roll(value, 64, 1).reshape(4, 16, 128)
    for x in range(8):
        o_ref[:, x, :] = ready[x].T[:64, :]

    for copy in swaps[0] + swaps[1] + spread_a[0] + spread_a[1] + spread_b[0] + spread_b[1] + ins + exchanges:
        copy.wait_send()

    @pl.when(s < 15)
    def _():
        up.wait_send()

    @pl.when(s > 0)
    def _():
        down.wait_send()

    for copy, away in backs:
        pl.when(away)(copy.wait_send)


def per_device(field, weight, bias):
    dma, chunks = pltpu.SemaphoreType.DMA, len(CHUNKS)
    result = pl.pallas_call(
        kernel,
        out_shape=jax.ShapeDtypeStruct((64, 8, 256), F32),
        in_specs=[pl.BlockSpec(memory_space=pltpu.HBM)] * 3,
        out_specs=pl.BlockSpec(memory_space=pltpu.VMEM),
        scratch_shapes=[
            pltpu.VMEM((64, 8, 256), F32),
            pltpu.VMEM((64,), F32),
            pltpu.VMEM((8, 272, 128), F32),
            pltpu.VMEM((8, 136, 128), F32),
            pltpu.VMEM((8, 136, 128), F32),
            pltpu.VMEM((4, 10, 48, 128), F32),
            pltpu.VMEM((4, 10, 32, 1152), BF16),
            pltpu.VMEM((28, 64, 256), F32),
            pltpu.VMEM((2, 28, 64, 128), F32),
            pltpu.VMEM((2, 9, 1152, 128), BF16),
            pltpu.VMEM((4, 2, 128, 256), F32),
            pltpu.VMEM((4, 128, 256), F32),
            pltpu.VMEM((4, 2, 2, 64, 128), F32),
            pltpu.VMEM((8, 2, 64, 128), F32),
            pltpu.VMEM((8, 256, 128), F32),
            dma((3,)),
            dma((2, chunks)),
            dma((2, chunks)),
            dma((2, chunks, 3)),
            dma((2, chunks, 3)),
            dma((2, chunks, 3)),
            dma((2, chunks, 3)),
            dma((2, 7)),
            dma((2, 8)),
            dma((2,)),
            dma((2,)),
            dma((4,)),
            dma((4,)),
            dma((4, 2, 2)),
            dma((8, 2)),
        ],
        compiler_params=pltpu.CompilerParams(
            collective_id=0, has_side_effects=True, vmem_limit_bytes=53 * 2**20
        ),
        cost_estimate=pl.CostEstimate(flops=4 * 10**9, bytes_accessed=4 * 10**6, transcendentals=131072),
        name="convolution",
    )(field.reshape(64, 8, 256), weight.reshape(27, 64, 256), bias)
    return result.reshape(64, 1, 8, 256)


def solution(mesh):
    placed = (P("chan", "filt", "space", None), P(None, None, None, "chan", None), P("filt"))
    return jax.shard_map(
        per_device,
        mesh=mesh,
        in_specs=placed,
        out_specs=P("filt", "chan", "space", None),
        check_vma=False,
    )
```

```python
import jax
import jax.numpy as jnp
from jax import lax
from jax.experimental import pallas as pl
from jax.experimental.pallas import tpu as pltpu
from jax.sharding import PartitionSpec as P

MESH = pl.DeviceIdType.MESH
CHUNKS = ((0, 8, 0), (14, 8, 1), (8, 6, 0), (22, 6, 1))
NEAR = (1, 7, 2, 6, 3, 5, 4)
ORDER = (0, 7, 1, 2, 3, 4, 5, 6)
F32, BF16 = jnp.float32, jnp.bfloat16


def split(value):
    high = value.astype(BF16)
    return high, (value - high.astype(F32)).astype(BF16)


def kernel(
    f_ref, w_ref, o_ref,
    field, turned, out_in, got_in, cells, taps, weight_own, weight_other, wcat, total, sibling, out_back, got_back, ready,
    own_sem, swap_ss, swap_rs, a_ss, a_rs, b_ss, b_rs, in_ss, in_rs, halo_ss, halo_rs, sib_ss, sib_rs, back_ss, back_rs,
):
    s, c, h = lax.axis_index("space"), lax.axis_index("chan"), lax.axis_index("filt")
    xx, yy = s // 4, s % 4
    lo, core = c // 2, c % 2
    z = 2 * h + lo

    def column(other_z, other_core):
        return (s, (other_z % 2) * 2 + other_core, other_z // 2)

    def plane(other_x, other_y):
        return (other_x * 4 + other_y, c, h)

    def remote(source, target, send, receive, device):
        return pltpu.make_async_remote_copy(
            source, target, send, receive, device_id=device, device_id_type=MESH
        )

    fetch_weight = pltpu.make_async_copy(w_ref, weight_own.at[pl.ds(0, 27)], own_sem.at[1])
    fetch_weight.start()
    fetch_field = pltpu.make_async_copy(f_ref, field, own_sem.at[0])
    fetch_field.start()

    barrier = pltpu.get_barrier_semaphore()
    greet = []
    for dz in range(8):
        for dk in range(2):
            if dz or dk:
                greet.append(column((z + dz) % 8, (core + dk) % 2))
    for d in range(1, 4):
        greet.append(plane((xx + d) % 4, yy))
        greet.append(plane(xx, (yy + d) % 4))
    greet.append(((s + 1) % 16, c, h))
    greet.append(((s + 15) % 16, c, h))
    for device in greet:
        pl.semaphore_signal(barrier, 1, device_id=device, device_id_type=MESH)

    lane = lax.broadcasted_iota(jnp.int32, (1, 128), 1)
    left = lane < 64

    weight_own[27] = jnp.zeros((64, 256), F32)
    fetch_weight.wait()
    pl.semaphore_wait(barrier, len(greet))

    def place(first, count, turn):
        u, v = (yy, xx) if turn else (xx, yy)
        rows = pl.multiple_of(16 * u + 8 * (v // 2), 8)
        return pl.ds(first + (count // 2) * (v % 2), count // 2), pl.ds(rows, 8)

    def piece(m, first, count, turn):
        own_taps, own_rows = place(first, count, turn)
        return weight_other.at[m, own_taps, own_rows, :]

    def band(m, first, count, turn):
        u = yy if turn else xx
        return weight_other.at[m, pl.ds(first, count), pl.ds(pl.multiple_of(16 * u, 16), 16), :]

    swaps = [[], []]

    def swap(m):
        for q, (first, count, turn) in enumerate(CHUNKS):
            target = (z + (7 if turn else 1)) % 8
            own_taps, own_rows = place(first, count, turn)
            lanes = pl.ds(pl.multiple_of(128 * ((target + target // 2 + target // 4 + m) % 2), 128), 128)
            copy = remote(
                weight_own.at[own_taps, own_rows, lanes], piece(m, first, count, turn),
                swap_ss.at[m, q], swap_rs.at[m, q], column(target, core),
            )
            copy.start()
            swaps[m].append(copy)

    swap(0)
    swap(1)

    fetch_field.wait()
    for x in range(8):
        rows = field[:, x, :]
        turned[x, 8:264, :] = jnp.concatenate([rows, rows], axis=0).T
        turned[x, 0:8, :] = jnp.zeros((8, 128), F32)
        turned[x, 264:272, :] = jnp.zeros((8, 128), F32)
    for t in range(8):
        base = 8 + 32 * t
        low_side = turned[:, base - 8 : base, :][:, 7, :]
        high_side = turned[:, base + 32 : base + 40, :][:, 0, :]
        out_in[t, 0:8, :] = jnp.where(left, low_side, high_side)
        for n, x in enumerate(ORDER):
            out_in[t, 8 + 16 * n : 24 + 16 * n, :] = jnp.where(
                left, turned[x, base : base + 16, :], turned[x, base + 16 : base + 32, :]
            )
    got_in[z] = out_in[z]

    @pl.when(s == 0)
    def _():
        cells[:, 0, :, :] = jnp.zeros((4, 48, 128), F32)

    @pl.when(s == 15)
    def _():
        cells[:, 9, :, :] = jnp.zeros((4, 48, 128), F32)


    PARTS = (pl.ds(0, 40), pl.ds(40, 96))
    ins = []
    for part in range(2):
        for n, dz in enumerate(NEAR):
            target = (z + dz) % 8
            ins.append(
                remote(
                    out_in.at[target, PARTS[part]], got_in.at[z, PARTS[part]],
                    in_ss.at[part, n], in_rs.at[part, z], column(target, core),
                )
            )
            ins[-1].start()

    def convert(m, half, first, count, read):
        @pl.loop(first, first + count)
        def _(tap):
            ab, y = tap // 3, tap % 3
            high, low = split(read(tap))
            for base, value in ((256 * y, high), (256 * y + 128, high), (768 + 128 * y, low)):
                wcat[m, ab, pl.ds(pl.multiple_of(base + 64 * half, 64), 64), :] = value

    spread_a, spread_b = [[], []], [[], []]

    def gather_a(m):
        for q, (first, count, turn) in enumerate(CHUNKS):
            swaps[m][q].wait_recv()
            for d in range(1, 4):
                target = plane((xx + d) % 4, yy) if turn else plane(xx, (yy + d) % 4)
                block = piece(m, first, count, turn)
                copy = remote(block, block, a_ss.at[m, q, d - 1], a_rs.at[m, q, d - 1], target)
                copy.start()
                spread_a[m].append(copy)

    def gather_b(m):
        for q, (first, count, turn) in enumerate(CHUNKS):
            for d in range(3):
                spread_a[m][3 * q + d].wait_recv()
            for d in range(1, 4):
                target = plane(xx, (yy + d) % 4) if turn else plane((xx + d) % 4, yy)
                block = band(m, first, count, turn)
                copy = remote(block, block, b_ss.at[m, q, d - 1], b_rs.at[m, q, d - 1], target)
                copy.start()
                spread_b[m].append(copy)

    def gathered(m):
        for q, (first, count, turn) in enumerate(CHUNKS):
            for d in range(3):
                spread_b[m][3 * q + d].wait_recv()
            convert(m, 1 - lo, first, min(count, 27 - first), lambda tap: weight_other[m, tap])

    gather_a(0)
    for j in range(2):
        convert((j + lo + h + h // 2) % 2, lo, 0, 27, lambda tap: weight_own[tap, :, 128 * j : 128 * j + 128])
    gather_b(0)
    gather_a(1)

    def arrived(part, p):
        for l in range(2):
            source = 2 * p + l

            @pl.when(source != z)
            def _():
                remote(
                    out_in.at[z, PARTS[part]], got_in.at[source, PARTS[part]],
                    in_ss.at[part, 0], in_rs.at[part, source], column(source, core),
                ).wait_recv()

    def unpack(p, n):
        x = ORDER[n]
        first = got_in[2 * p, 8 + 16 * n : 24 + 16 * n, :]
        second = got_in[2 * p + 1, 8 + 16 * n : 24 + 16 * n, :]
        cells[p, 1 + x, 8:24, :] = jnp.where(left, first, pltpu.roll(second, 64, 1))
        cells[p, 1 + x, 24:40, :] = jnp.where(left, pltpu.roll(first, 64, 1), second)

    def spread(p, x):
        for y in range(3):
            high, low = split(cells[p, x, 7 + y : 39 + y, :])
            taps[p, x, :, 256 * y : 256 * y + 128] = high
            taps[p, x, :, 256 * y + 128 : 256 * y + 256] = low
            taps[p, x, :, 768 + 128 * y : 896 + 128 * y] = high

    def boundary(p):
        arrived(0, p)
        first = got_in[2 * p, 0:8, :]
        second = got_in[2 * p + 1, 0:8, :]
        low_side = jnp.where(left, first, pltpu.roll(second, 64, 1))
        high_side = jnp.where(left, pltpu.roll(first, 64, 1), second)
        for x in range(8):
            cells[p, 1 + x, 7:8, :] = low_side[x : x + 1]
            cells[p, 1 + x, 40:41, :] = high_side[x : x + 1]
        unpack(p, 0)
        unpack(p, 1)

    def inside(p):
        arrived(1, p)
        for n in range(2, 8):
            unpack(p, n)

        @pl.loop(1, 9)
        def _(x):
            spread(p, x)

    planes = [(h + d) % 4 for d in (0, 1, 3, 2)]

    @pl.loop(0, 4)
    def _(n):
        boundary((h + n) % 4)

    up = remote(cells.at[:, 8], cells.at[:, 0], halo_ss.at[0], halo_rs.at[0], ((s + 1) % 16, c, h))
    down = remote(cells.at[:, 1], cells.at[:, 9], halo_ss.at[1], halo_rs.at[1], ((s + 15) % 16, c, h))

    @pl.when(s < 15)
    def _():
        up.start()

    @pl.when(s > 0)
    def _():
        down.start()

    gathered(0)
    gather_b(1)
    for p in planes:
        inside(p)

    @pl.when(s > 0)
    def _():
        up.wait_recv()

    @pl.when(s < 15)
    def _():
        down.wait_recv()

    @pl.loop(0, 4)
    def _(p):
        spread(p, 0)
        spread(p, 9)

    def left_side(part, p):
        return jnp.concatenate([taps[p, pl.ds(4 * part + b, 4)].reshape(128, 1152) for b in range(3)], axis=1)

    def right_side(m, a):
        return wcat[m, pl.ds(3 * a, 3)].reshape(3456, 128)

    def convolve(target, part, m, g):
        onward = 2 - 2 * g
        middle, ahead = right_side(m, 1), right_side(m, onward)
        target[...] = jnp.dot(
            jnp.concatenate([left_side(part, 3 * g), left_side(part, 1 + g)], axis=1),
            jnp.concatenate(
                [
                    jnp.concatenate([middle, right_side(m, 2 - onward)], axis=1),
                    jnp.concatenate([ahead, middle], axis=1),
                ],
                axis=0,
            ),
            preferred_element_type=F32,
        )
        target[:, 128:] += jnp.dot(left_side(part, 2 - g), ahead, preferred_element_type=F32)

    exchanges, backs = [], []

    def begin(part, m):
        k = 2 * m + part
        convolve(total.at[k, 0], part, m, 1 - core)
        exchange = remote(total.at[k, 0], sibling.at[k], sib_ss.at[k], sib_rs.at[k], column(z, 1 - core))
        exchange.start()
        exchanges.append(exchange)

    def finish(part, m):
        k = 2 * m + part
        convolve(total.at[k, 1], part, m, core)
        exchanges[k].wait_recv()

        for n in range(2):
            p = 1 + core if n else 3 * core
            lanes = slice(128 * n, 128 * n + 128)
            value = (total[k, 1, :, lanes] + sibling[k, :, lanes]).reshape(4, 32, 128)
            low_part = value[:, :16, :].reshape(64, 128)
            high_part = value[:, 16:, :].reshape(64, 128)
            out_back[k, n, 0] = jnp.where(left, low_part, pltpu.roll(high_part, 64, 1))
            out_back[k, n, 1] = jnp.where(left, pltpu.roll(low_part, 64, 1), high_part)
            for j in range(2):
                f = 2 * ((lo + h + h // 2 + m) % 2) + j
                away = jnp.logical_or(p != c, f != h)
                block, place_back = out_back.at[k, n, j], got_back.at[z, part]
                copy = remote(block, place_back, back_ss.at[k, n, j], back_rs.at[z, part], (s, p, f))
                here = pltpu.make_async_copy(block, place_back, back_rs.at[z, part])
                pl.when(away)(copy.start)
                pl.when(jnp.logical_not(away))(here.start)
                backs.append((copy, away))

    for m in range(2):
        if m:
            gathered(m)
        begin(0, m)
        begin(1, m)
        finish(0, m)
        finish(1, m)

    for n in range(16):
        source, part = 2 * (n % 4) + (h // 2 + n % 4 + n % 4 // 2 + n // 8) % 2, n // 4 % 2
        arrival = got_back.at[source, part]
        pltpu.make_async_copy(arrival, arrival, back_rs.at[source, part]).wait()
        value = got_back[source, part]
        rows, columns = pl.multiple_of(32 * source, 32), slice(4 * part, 4 * part + 4)
        ready[columns, pl.ds(rows, 16), :] = value.reshape(4, 16, 128)
        ready[columns, pl.ds(rows + 16, 16), :] = pltpu.roll(value, 64, 1).reshape(4, 16, 128)
    for x in range(8):
        o_ref[:, x, :] = ready[x].T[:64, :]

    for copy in swaps[0] + swaps[1] + spread_a[0] + spread_a[1] + spread_b[0] + spread_b[1] + ins + exchanges:
        copy.wait_send()

    @pl.when(s < 15)
    def _():
        up.wait_send()

    @pl.when(s > 0)
    def _():
        down.wait_send()

    for copy, away in backs:
        pl.when(away)(copy.wait_send)


def per_device(field, weight, bias):
    dma, chunks = pltpu.SemaphoreType.DMA, len(CHUNKS)
    result = pl.pallas_call(
        kernel,
        out_shape=jax.ShapeDtypeStruct((64, 8, 256), F32),
        in_specs=[pl.BlockSpec(memory_space=pltpu.HBM)] * 2,
        out_specs=pl.BlockSpec(memory_space=pltpu.VMEM),
        scratch_shapes=[
            pltpu.VMEM((64, 8, 256), F32),
            pltpu.VMEM((8, 272, 128), F32),
            pltpu.VMEM((8, 136, 128), F32),
            pltpu.VMEM((8, 136, 128), F32),
            pltpu.VMEM((4, 10, 48, 128), F32),
            pltpu.VMEM((4, 10, 32, 1152), BF16),
            pltpu.VMEM((28, 64, 256), F32),
            pltpu.VMEM((2, 28, 64, 128), F32),
            pltpu.VMEM((2, 9, 1152, 128), BF16),
            pltpu.VMEM((4, 2, 128, 256), F32),
            pltpu.VMEM((4, 128, 256), F32),
            pltpu.VMEM((4, 2, 2, 64, 128), F32),
            pltpu.VMEM((8, 2, 64, 128), F32),
            pltpu.VMEM((8, 256, 128), F32),
            dma((2,)),
            dma((2, chunks)),
            dma((2, chunks)),
            dma((2, chunks, 3)),
            dma((2, chunks, 3)),
            dma((2, chunks, 3)),
            dma((2, chunks, 3)),
            dma((2, 7)),
            dma((2, 8)),
            dma((2,)),
            dma((2,)),
            dma((4,)),
            dma((4,)),
            dma((4, 2, 2)),
            dma((8, 2)),
        ],
        compiler_params=pltpu.CompilerParams(
            collective_id=0, has_side_effects=True, vmem_limit_bytes=53 * 2**20
        ),
        cost_estimate=pl.CostEstimate(flops=4 * 10**9, bytes_accessed=4 * 10**6, transcendentals=131072),
        name="convolution",
    )(field.reshape(64, 8, 256), weight.reshape(27, 64, 256))
    return jax.nn.silu(result.reshape(64, 1, 8, 256) + bias[:, None, None, None])


def solution(mesh):
    placed = (P("chan", "filt", "space", None), P(None, None, None, "chan", None), P("filt"))
    return jax.shard_map(
        per_device,
        mesh=mesh,
        in_specs=placed,
        out_specs=P("filt", "chan", "space", None),
        check_vma=False,
    )
```

```python
import jax
import jax.numpy as jnp
from jax import lax
from jax.experimental import pallas as pl
from jax.experimental.pallas import tpu as pltpu
from jax.sharding import PartitionSpec as P

MESH = pl.DeviceIdType.MESH
CHUNKS = ((0, 8, 0), (14, 8, 1), (8, 6, 0), (22, 6, 1))
NEAR = (1, 7, 2, 6, 3, 5, 4)
ORDER = (0, 7, 1, 2, 3, 4, 5, 6)
F32, BF16 = jnp.float32, jnp.bfloat16


def split(value):
    high = value.astype(BF16)
    return high, (value - high.astype(F32)).astype(BF16)


def kernel(
    f_ref, w_ref, o_ref,
    field, turned, out_in, got_in, cells, taps, weight_own, weight_other, wcat, total, sibling, out_back, got_back, ready,
    own_sem, swap_ss, swap_rs, a_ss, a_rs, b_ss, b_rs, in_ss, in_rs, halo_ss, halo_rs, sib_ss, sib_rs, back_ss, back_rs,
):
    s, c, h = lax.axis_index("space"), lax.axis_index("chan"), lax.axis_index("filt")
    xx, yy = s // 4, s % 4
    lo, core = c // 2, c % 2
    z = 2 * h + lo

    def column(other_z, other_core):
        return (s, (other_z % 2) * 2 + other_core, other_z // 2)

    def plane(other_x, other_y):
        return (other_x * 4 + other_y, c, h)

    def remote(source, target, send, receive, device):
        return pltpu.make_async_remote_copy(
            source, target, send, receive, device_id=device, device_id_type=MESH
        )

    fetch_weight = pltpu.make_async_copy(w_ref, weight_own.at[pl.ds(0, 27)], own_sem.at[1])
    fetch_weight.start()
    fetch_field = pltpu.make_async_copy(f_ref, field, own_sem.at[0])
    fetch_field.start()

    barrier = pltpu.get_barrier_semaphore()
    greet = []
    for dz in range(8):
        for dk in range(2):
            if dz or dk:
                greet.append(column((z + dz) % 8, (core + dk) % 2))
    for d in range(1, 4):
        greet.append(plane((xx + d) % 4, yy))
        greet.append(plane(xx, (yy + d) % 4))
    greet.append(((s + 1) % 16, c, h))
    greet.append(((s + 15) % 16, c, h))
    for device in greet:
        pl.semaphore_signal(barrier, 1, device_id=device, device_id_type=MESH)

    lane = lax.broadcasted_iota(jnp.int32, (1, 128), 1)
    left = lane < 64

    weight_own[27] = jnp.zeros((64, 256), F32)
    fetch_weight.wait()
    pl.semaphore_wait(barrier, len(greet))

    def place(first, count, turn):
        u, v = (yy, xx) if turn else (xx, yy)
        rows = pl.multiple_of(16 * u + 8 * (v // 2), 8)
        return pl.ds(first + (count // 2) * (v % 2), count // 2), pl.ds(rows, 8)

    def piece(m, first, count, turn):
        own_taps, own_rows = place(first, count, turn)
        return weight_other.at[m, own_taps, own_rows, :]

    def band(m, first, count, turn):
        u = yy if turn else xx
        return weight_other.at[m, pl.ds(first, count), pl.ds(pl.multiple_of(16 * u, 16), 16), :]

    swaps = [[], []]

    def swap(m):
        for q, (first, count, turn) in enumerate(CHUNKS):
            target = (z + (7 if turn else 1)) % 8
            own_taps, own_rows = place(first, count, turn)
            lanes = pl.ds(pl.multiple_of(128 * ((target + target // 2 + target // 4 + m) % 2), 128), 128)
            copy = remote(
                weight_own.at[own_taps, own_rows, lanes], piece(m, first, count, turn),
                swap_ss.at[m, q], swap_rs.at[m, q], column(target, core),
            )
            copy.start()
            swaps[m].append(copy)

    swap(0)
    swap(1)

    fetch_field.wait()
    for x in range(8):
        rows = field[:, x, :]
        turned[x, 8:264, :] = jnp.concatenate([rows, rows], axis=0).T
        turned[x, 0:8, :] = jnp.zeros((8, 128), F32)
        turned[x, 264:272, :] = jnp.zeros((8, 128), F32)
    for t in range(8):
        base = 8 + 32 * t
        low_side = turned[:, base - 8 : base, :][:, 7, :]
        high_side = turned[:, base + 32 : base + 40, :][:, 0, :]
        out_in[t, 0:8, :] = jnp.where(left, low_side, high_side)
        for n, x in enumerate(ORDER):
            out_in[t, 8 + 16 * n : 24 + 16 * n, :] = jnp.where(
                left, turned[x, base : base + 16, :], turned[x, base + 16 : base + 32, :]
            )
    got_in[z] = out_in[z]

    @pl.when(s == 0)
    def _():
        cells[:, 0, :, :] = jnp.zeros((4, 48, 128), F32)

    @pl.when(s == 15)
    def _():
        cells[:, 9, :, :] = jnp.zeros((4, 48, 128), F32)


    PARTS = (pl.ds(0, 40), pl.ds(40, 96))
    ins = []
    for part in range(2):
        for n, dz in enumerate(NEAR):
            target = (z + dz) % 8
            ins.append(
                remote(
                    out_in.at[target, PARTS[part]], got_in.at[z, PARTS[part]],
                    in_ss.at[part, n], in_rs.at[part, z], column(target, core),
                )
            )
            ins[-1].start()

    def convert(m, half, first, count, read):
        @pl.loop(first, first + count)
        def _(tap):
            ab, y = tap // 3, tap % 3
            high, low = split(read(tap))
            for base, value in ((256 * y, high), (256 * y + 128, high), (768 + 128 * y, low)):
                wcat[m, ab, pl.ds(pl.multiple_of(base + 64 * half, 64), 64), :] = value

    spread_a, spread_b = [[], []], [[], []]

    def gather_a(m):
        for q, (first, count, turn) in enumerate(CHUNKS):
            swaps[m][q].wait_recv()
            for d in range(1, 4):
                target = plane((xx + d) % 4, yy) if turn else plane(xx, (yy + d) % 4)
                block = piece(m, first, count, turn)
                copy = remote(block, block, a_ss.at[m, q, d - 1], a_rs.at[m, q, d - 1], target)
                copy.start()
                spread_a[m].append(copy)

    def gather_b(m):
        for q, (first, count, turn) in enumerate(CHUNKS):
            for d in range(3):
                spread_a[m][3 * q + d].wait_recv()
            for d in range(1, 4):
                target = plane(xx, (yy + d) % 4) if turn else plane((xx + d) % 4, yy)
                block = band(m, first, count, turn)
                copy = remote(block, block, b_ss.at[m, q, d - 1], b_rs.at[m, q, d - 1], target)
                copy.start()
                spread_b[m].append(copy)

    def gathered(m):
        for q, (first, count, turn) in enumerate(CHUNKS):
            for d in range(3):
                spread_b[m][3 * q + d].wait_recv()
            convert(m, 1 - lo, first, min(count, 27 - first), lambda tap: weight_other[m, tap])

    gather_a(0)
    for j in range(2):
        convert((j + lo + h + h // 2) % 2, lo, 0, 27, lambda tap: weight_own[tap, :, 128 * j : 128 * j + 128])
    gather_b(0)
    gather_a(1)

    def arrived(part, p):
        for l in range(2):
            source = 2 * p + l

            @pl.when(source != z)
            def _():
                remote(
                    out_in.at[z, PARTS[part]], got_in.at[source, PARTS[part]],
                    in_ss.at[part, 0], in_rs.at[part, source], column(source, core),
                ).wait_recv()

    def unpack(p, n):
        x = ORDER[n]
        first = got_in[2 * p, 8 + 16 * n : 24 + 16 * n, :]
        second = got_in[2 * p + 1, 8 + 16 * n : 24 + 16 * n, :]
        cells[p, 1 + x, 8:24, :] = jnp.where(left, first, pltpu.roll(second, 64, 1))
        cells[p, 1 + x, 24:40, :] = jnp.where(left, pltpu.roll(first, 64, 1), second)

    def spread(p, x):
        for y in range(3):
            high, low = split(cells[p, x, 7 + y : 39 + y, :])
            taps[p, x, :, 256 * y : 256 * y + 128] = high
            taps[p, x, :, 256 * y + 128 : 256 * y + 256] = low
            taps[p, x, :, 768 + 128 * y : 896 + 128 * y] = high

    def boundary(p):
        arrived(0, p)
        first = got_in[2 * p, 0:8, :]
        second = got_in[2 * p + 1, 0:8, :]
        low_side = jnp.where(left, first, pltpu.roll(second, 64, 1))
        high_side = jnp.where(left, pltpu.roll(first, 64, 1), second)
        for x in range(8):
            cells[p, 1 + x, 7:8, :] = low_side[x : x + 1]
            cells[p, 1 + x, 40:41, :] = high_side[x : x + 1]
        unpack(p, 0)
        unpack(p, 1)

    def inside(p):
        arrived(1, p)
        for n in range(2, 8):
            unpack(p, n)

        @pl.loop(1, 9)
        def _(x):
            spread(p, x)

    planes = [(h + d) % 4 for d in (0, 1, 3, 2)]

    @pl.loop(0, 4)
    def _(n):
        boundary((h + n) % 4)

    up = remote(cells.at[:, 8], cells.at[:, 0], halo_ss.at[0], halo_rs.at[0], ((s + 1) % 16, c, h))
    down = remote(cells.at[:, 1], cells.at[:, 9], halo_ss.at[1], halo_rs.at[1], ((s + 15) % 16, c, h))

    @pl.when(s < 15)
    def _():
        up.start()

    @pl.when(s > 0)
    def _():
        down.start()

    gathered(0)
    gather_b(1)
    for p in planes:
        inside(p)

    def left_side(part, p):
        def shifted(b):
            if part == 0:
                return taps[p, pl.ds(2 + b, 4)].reshape(128, 1152)
            ends = [taps[p, pl.ds(6 * n + b, 2)].reshape(64, 1152) for n in range(2)]
            return jnp.concatenate(ends, axis=0)

        return jnp.concatenate([shifted(b) for b in range(3)], axis=1)

    def right_side(m, a):
        return wcat[m, pl.ds(3 * a, 3)].reshape(3456, 128)

    def convolve(target, part, m, g):
        onward = 2 - 2 * g
        middle, ahead = right_side(m, 1), right_side(m, onward)
        target[...] = jnp.dot(
            jnp.concatenate([left_side(part, 3 * g), left_side(part, 1 + g)], axis=1),
            jnp.concatenate(
                [
                    jnp.concatenate([middle, right_side(m, 2 - onward)], axis=1),
                    jnp.concatenate([ahead, middle], axis=1),
                ],
                axis=0,
            ),
            preferred_element_type=F32,
        )
        target[:, 128:] += jnp.dot(left_side(part, 2 - g), ahead, preferred_element_type=F32)

    exchanges, backs = [], []

    def begin(part, m):
        k = 2 * m + part
        convolve(total.at[k, 0], part, m, 1 - core)
        exchange = remote(total.at[k, 0], sibling.at[k], sib_ss.at[k], sib_rs.at[k], column(z, 1 - core))
        exchange.start()
        exchanges.append(exchange)

    def finish(part, m):
        k = 2 * m + part
        convolve(total.at[k, 1], part, m, core)
        exchanges[k].wait_recv()

        for n in range(2):
            p = 1 + core if n else 3 * core
            lanes = slice(128 * n, 128 * n + 128)
            value = (total[k, 1, :, lanes] + sibling[k, :, lanes]).reshape(4, 32, 128)
            low_part = value[:, :16, :].reshape(64, 128)
            high_part = value[:, 16:, :].reshape(64, 128)
            out_back[k, n, 0] = jnp.where(left, low_part, pltpu.roll(high_part, 64, 1))
            out_back[k, n, 1] = jnp.where(left, pltpu.roll(low_part, 64, 1), high_part)
            for j in range(2):
                f = 2 * ((lo + h + h // 2 + m) % 2) + j
                away = jnp.logical_or(p != c, f != h)
                block, place_back = out_back.at[k, n, j], got_back.at[z, part]
                copy = remote(block, place_back, back_ss.at[k, n, j], back_rs.at[z, part], (s, p, f))
                here = pltpu.make_async_copy(block, place_back, back_rs.at[z, part])
                pl.when(away)(copy.start)
                pl.when(jnp.logical_not(away))(here.start)
                backs.append((copy, away))

    for m in range(2):
        if m:
            gathered(m)
        begin(0, m)
        if m == 0:
            @pl.when(s > 0)
            def _():
                up.wait_recv()

            @pl.when(s < 15)
            def _():
                down.wait_recv()

            @pl.loop(0, 4)
            def _(p):
                spread(p, 0)
                spread(p, 9)

        begin(1, m)
        finish(0, m)
        finish(1, m)

    for n in range(16):
        source, part = 2 * (n % 4) + (h // 2 + n % 4 + n % 4 // 2 + n // 8) % 2, n // 4 % 2
        arrival = got_back.at[source, part]
        pltpu.make_async_copy(arrival, arrival, back_rs.at[source, part]).wait()
        value = got_back[source, part]
        rows = pl.multiple_of(32 * source, 32)
        value, other = value.reshape(4, 16, 128), pltpu.roll(value, 64, 1).reshape(4, 16, 128)
        for place_x, own_x in (((2, 0),) if part == 0 else ((0, 0), (6, 2))):
            width = 2 if part else 4
            ready[place_x : place_x + width, pl.ds(rows, 16), :] = value[own_x : own_x + width]
            ready[place_x : place_x + width, pl.ds(rows + 16, 16), :] = other[own_x : own_x + width]
    for x in range(8):
        o_ref[:, x, :] = ready[x].T[:64, :]

    for copy in swaps[0] + swaps[1] + spread_a[0] + spread_a[1] + spread_b[0] + spread_b[1] + ins + exchanges:
        copy.wait_send()

    @pl.when(s < 15)
    def _():
        up.wait_send()

    @pl.when(s > 0)
    def _():
        down.wait_send()

    for copy, away in backs:
        pl.when(away)(copy.wait_send)


def per_device(field, weight, bias):
    dma, chunks = pltpu.SemaphoreType.DMA, len(CHUNKS)
    result = pl.pallas_call(
        kernel,
        out_shape=jax.ShapeDtypeStruct((64, 8, 256), F32),
        in_specs=[pl.BlockSpec(memory_space=pltpu.HBM)] * 2,
        out_specs=pl.BlockSpec(memory_space=pltpu.VMEM),
        scratch_shapes=[
            pltpu.VMEM((64, 8, 256), F32),
            pltpu.VMEM((8, 272, 128), F32),
            pltpu.VMEM((8, 136, 128), F32),
            pltpu.VMEM((8, 136, 128), F32),
            pltpu.VMEM((4, 10, 48, 128), F32),
            pltpu.VMEM((4, 10, 32, 1152), BF16),
            pltpu.VMEM((28, 64, 256), F32),
            pltpu.VMEM((2, 28, 64, 128), F32),
            pltpu.VMEM((2, 9, 1152, 128), BF16),
            pltpu.VMEM((4, 2, 128, 256), F32),
            pltpu.VMEM((4, 128, 256), F32),
            pltpu.VMEM((4, 2, 2, 64, 128), F32),
            pltpu.VMEM((8, 2, 64, 128), F32),
            pltpu.VMEM((8, 256, 128), F32),
            dma((2,)),
            dma((2, chunks)),
            dma((2, chunks)),
            dma((2, chunks, 3)),
            dma((2, chunks, 3)),
            dma((2, chunks, 3)),
            dma((2, chunks, 3)),
            dma((2, 7)),
            dma((2, 8)),
            dma((2,)),
            dma((2,)),
            dma((4,)),
            dma((4,)),
            dma((4, 2, 2)),
            dma((8, 2)),
        ],
        compiler_params=pltpu.CompilerParams(
            collective_id=0, has_side_effects=True, vmem_limit_bytes=53 * 2**20
        ),
        cost_estimate=pl.CostEstimate(flops=4 * 10**9, bytes_accessed=4 * 10**6, transcendentals=131072),
        name="convolution",
    )(field.reshape(64, 8, 256), weight.reshape(27, 64, 256))
    return jax.nn.silu(result.reshape(64, 1, 8, 256) + bias[:, None, None, None])


def solution(mesh):
    placed = (P("chan", "filt", "space", None), P(None, None, None, "chan", None), P("filt"))
    return jax.shard_map(
        per_device,
        mesh=mesh,
        in_specs=placed,
        out_specs=P("filt", "chan", "space", None),
        check_vma=False,
    )
```
